256 devices in a mesh: tm: 8 (over y, core), mp: 4 (over z_lo), tok: 8 (over z_hi, x).
Axes of the slice: x: 4, y: 4, z: 8 (z_hi: 2, z_lo: 4; z = z_hi * 4 + z_lo), core: 2. Of those that a mesh axis runs over, the one named last changes fastest.
Arguments:
- features: bfloat16 [1024, 3584], P('tok'), may hold values from -6 to 6
- spike_mask: int32 [8, 1024, 3584], P('tm', 'tok'), may hold values 0 or 1
- gate_weight: bfloat16 [3584, 7168], P(('tm', 'tok'), 'mp'), may hold values from -0.09375 to 0.09375
- threshold: float32 [7168], P('mp'), may hold values from 0.5 to 2
Outputs:
- rates: float32 [1024, 7168], P('tok', 'mp')
- grad_threshold: float32 [7168], P('mp')
The draws below stay inside these ranges and needn't reach their ends.
All inputs are finite; a program needn't handle non-finite values. No bound on the sum of `spike_mask` on one device may be relied on, other than what follows from the above.
Results may differ from the reference program's by a relative error of at most 0.00035.
Values may be sent and summed in bfloat16 or wider, within the bound.
No kernel may reach another device: no remote copies, remote signals or barrier semaphores. Data moves between devices by JAX's collectives and lax.ppermute only.
A program may use at most 64 MiB of HBM per device.

```python
import math
import jax
import jax.numpy as jnp
from jax import lax

D = 3584
FF = 7168
STEPS = 8
TOKENS = 1024


def plant(entries, key, low, top_value):
    dims = entries.shape
    spot = [jax.random.randint(jax.random.fold_in(key, axis), (), 0, dims[axis]) for axis in range(len(dims))]
    entries = entries.at[tuple(spot)].set(low)
    longest = dims.index(max(dims))
    spot[longest] = (spot[longest] + 1) % dims[longest]
    return entries.at[tuple(spot)].set(top_value)


def shard_levels(own_key, extent, shards, low, largest):
    gain = 1.0
    for axis_at, parts in shards:
        heights = jax.random.uniform(jax.random.fold_in(jax.random.fold_in(own_key, 6), axis_at), (parts,), jnp.float32, low / len(shards), largest / len(shards))
        gain = gain * jnp.repeat(jnp.exp(heights), extent[axis_at] // parts).reshape((-1,) + (1,) * (len(extent) - 1 - axis_at))
    return gain


def scatter_about(rng, dims, spread, most, pieces=(), held_as=jnp.bfloat16):
    values = spread * jax.random.normal(rng, dims, jnp.float32)
    if pieces:
        values = values * shard_levels(rng, dims, pieces, -0.22, 0.18)
    return jnp.clip(values, -most, most).astype(held_as)


def setup_inputs(seed: int = 0) -> dict:
    seeds = jax.random.split(jax.random.key(seed), 5)
    return {
        "features": scatter_about(seeds[0], (TOKENS, D), 1.0, 6.0, ((0, 8),)),
        "spike_mask": plant((jax.random.randint(seeds[1], (STEPS, TOKENS, D), 0, 2) < 1).astype(jnp.int32), jax.random.fold_in(seeds[1], 1), 0, 1),
        "gate_weight": scatter_about(seeds[2], (D, FF), D ** -0.5, 0.09375, ((0, 64), (1, 4))),
        "threshold": jnp.clip(jnp.exp(math.log(2.0) - 1.3862944 * jax.random.uniform(seeds[3], (FF,), jnp.float32) ** shard_levels(seeds[3], (FF,), ((0, 4),), -0.2, 0.2)), 0.5, 2.0),
    }


SHARP = 2.0


def reference(features, spike_mask, gate_weight, threshold):
    target = jax.nn.silu(jnp.dot(features, gate_weight, preferred_element_type=jnp.float32))
    empty = jnp.zeros(target.shape, jnp.float32)

    def forward(potential, mask_step):
        driven = jnp.where(mask_step > 0, features, jnp.zeros_like(features))
        current = 2.0 * jnp.dot(driven, gate_weight, preferred_element_type=jnp.float32)
        rising = potential + current
        fired = jax.nn.sigmoid(SHARP * (rising - threshold))
        return rising - threshold * fired, fired

    final_state, fired_all = lax.scan(forward, empty, spike_mask)
    total = jnp.sum(fired_all, axis=0)
    rates = threshold * total / STEPS
    error = (rates - target) / TOKENS

    def backward(carry, fired):
        cotangent, grad_sum = carry
        dspike = error * threshold / STEPS - threshold * cotangent
        dwide = dspike * SHARP * fired * (1.0 - fired)
        term = jnp.sum(-dwide - fired * cotangent + error * fired / STEPS, axis=0)
        return (cotangent + dwide, grad_sum + term), None

    start = (empty, jnp.zeros(threshold.shape, jnp.float32))
    (last_cot, grad_threshold), unused = lax.scan(backward, start, fired_all, reverse=True)
    return rates, grad_threshold
```

```python
import functools
import jax
import jax.numpy as jnp
from jax import lax
from jax.experimental import pallas as pl
from jax.experimental.pallas import tpu as pltpu
from jax.sharding import Mesh, PartitionSpec as P

SHARP = 2.0
STARTS = (0, 384, 896, 1280)
WIDE = 512
Y, CORE, Z, X = 4, 2, 2, 4
STEPS = Y * CORE


def around(x, axis, by):
    n = lax.axis_size(axis)
    return lax.ppermute(x, axis, [(i, (i + by) % n) for i in range(n)])


def student_kernel(core_ref, driven_ref, features_ref, mine_ref, other_ref, threshold_ref, rates_ref, grad_ref, current_ref, teacher_ref, *, tokens_all):
    rows = features_ref.shape[0]
    depth = mine_ref.shape[1]
    first = core_ref[0] == 0
    chunk = 2 * depth
    for n in range(0, WIDE, 256):
        total = jnp.zeros((STEPS * rows, 256), jnp.float32)
        teacher = jnp.zeros((rows, 256), jnp.float32)
        for y in range(Y):
            mine = mine_ref[y, :, n : n + 256]
            other = other_ref[y, :, n : n + 256]
            weight = jnp.concatenate(
                [jnp.where(first, mine, other), jnp.where(first, other, mine)], axis=0
            )
            left = driven_ref[:, :, y * chunk : (y + 1) * chunk].reshape(STEPS * rows, chunk)
            total = total + jnp.dot(left, weight, preferred_element_type=jnp.float32)
            teacher = teacher + jnp.dot(
                features_ref[:, y * chunk : (y + 1) * chunk], weight, preferred_element_type=jnp.float32
            )
        current_ref[:, :, n : n + 256] = total.reshape(STEPS, rows, 256)
        teacher_ref[:, n : n + 256] = teacher
    threshold = threshold_ref[...]
    tall = 8

    def strip(i, grad_sum):
        at = pl.ds(pl.multiple_of(i * tall, tall), tall)
        potential = jnp.zeros((tall, WIDE), jnp.float32)
        spikes = []
        for t in range(STEPS):
            rising = potential + 2.0 * current_ref[t, at, :]
            fired = jax.nn.sigmoid(SHARP * (rising - threshold))
            potential = rising - threshold * fired
            spikes.append(fired)
        total = spikes[0]
        for t in range(1, STEPS):
            total = total + spikes[t]
        rates = threshold * total / STEPS
        rates_ref[at, :] = rates
        v = teacher_ref[at, :]
        error = (rates - v * jax.nn.sigmoid(v)) / tokens_all
        cotangent = jnp.zeros((tall, WIDE), jnp.float32)
        for t in reversed(range(STEPS)):
            fired = spikes[t]
            dspike = error * threshold / STEPS - threshold * cotangent
            dwide = dspike * SHARP * fired * (1.0 - fired)
            grad_sum = grad_sum + (-dwide - fired * cotangent + error * fired / STEPS)
            cotangent = cotangent + dwide
        return grad_sum

    grad_sum = lax.fori_loop(0, rows // tall, strip, jnp.zeros((tall, WIDE), jnp.float32))
    grad_ref[...] = jnp.sum(grad_sum, axis=0, keepdims=True)


def place_kernel(at_ref, *refs):
    out_ref = refs[-1]
    half = out_ref.shape[0] // 2
    core, y = at_ref[0], at_ref[1]
    for j in range(Y):
        source = (y + j) % Y
        start = pl.multiple_of(jnp.where(source < 2, 0, 896) + jnp.where(source % 2 == 1, 384, 0), 128)
        for k in range(CORE):
            row = pl.multiple_of(((core + k) % CORE) * half, half)
            piece = refs[CORE * j + k]

            @pl.when(source % 2 == 0)
            def _():
                out_ref[pl.ds(row, half), pl.ds(start, WIDE)] = piece[...]

            @pl.when(source % 2 == 1)
            def _():
                out_ref[pl.ds(row, half), pl.ds(start + 128, WIDE - 128)] = piece[:, 128:]


def on_device(features, spike_mask, gate_weight, threshold):
    core, y, x = lax.axis_index("core"), lax.axis_index("y"), lax.axis_index("x")
    rows, deep = features.shape
    tokens_all = rows * Z * X
    half = rows // CORE
    part, width = gate_weight.shape

    def other_core(v):
        return around(v, "core", 1)

    def tokens_of(v, which):
        return lax.dynamic_slice_in_dim(v, which * half, half, axis=0)

    mine_f = tokens_of(features, core)

    def drive(which):
        return jnp.where(tokens_of(spike_mask[0], which) > 0, tokens_of(features, which), jnp.zeros((), features.dtype))

    give = drive(1 - core)
    keep = drive(core)

    windows = jnp.stack([gate_weight[:, s : s + WIDE] for s in STARTS])
    payload = jnp.concatenate([windows] * Z)
    landed = lax.all_to_all(payload, ("z", "y"), 0, 0, tiled=True)
    wa, wb = landed[:Y], landed[Y:]

    got = other_core(give)
    keep_p, keep_m = around(keep, "y", 1), around(keep, "y", -1)
    got_p, got_m = around(got, "y", 1), around(got, "y", -1)
    keep_f = around(keep_p, "y", 1)
    got_f = around(got_m, "y", -1)

    wa_p, wa_m = around(wa, "x", 1), around(wa, "x", -1)
    wb_p, wb_m = around(wb, "x", 1), around(wb, "x", -1)
    wa_f = around(wa_p, "x", 1)
    wb_f = around(wb_m, "x", -1)

    driven = jnp.zeros((STEPS, half, deep), features.dtype)
    for piece, dy, dc in (
        (keep, 0, 0), (got, 0, 1), (keep_p, -1, 0), (got_p, -1, 1),
        (keep_m, 1, 0), (got_m, 1, 1), (keep_f, 2, 0), (got_f, 2, 1),
    ):
        step = lax.rem(y + dy + Y, Y) * CORE + lax.rem(core + dc, CORE)
        driven = lax.dynamic_update_slice(driven, piece[None], (step, 0, 0))

    mine = jnp.zeros((Y, Z, X, part, WIDE), gate_weight.dtype)
    theirs = jnp.zeros((Y, Z, X, part, WIDE), gate_weight.dtype)
    for piece, z, dx in (
        (wa, 0, 0), (wb, 1, 0), (wa_p, 0, -1), (wb_p, 1, -1),
        (wa_m, 0, 1), (wb_m, 1, 1), (wa_f, 0, 2), (wb_f, 1, 2),
    ):
        at = (0, z, lax.rem(x + dx + X, X), 0, 0)
        mine = lax.dynamic_update_slice(mine, piece[:, None, None], at)
        theirs = lax.dynamic_update_slice(theirs, other_core(piece)[:, None, None], at)
    mine = mine.reshape(Y, Z * X * part, WIDE)
    theirs = theirs.reshape(Y, Z * X * part, WIDE)

    start = jnp.asarray(STARTS, jnp.int32)[y]
    own_threshold = lax.dynamic_slice_in_dim(threshold, start, WIDE)[None]

    smem = pl.BlockSpec(memory_space=pltpu.SMEM)
    vmem = pl.BlockSpec(memory_space=pltpu.VMEM)
    rates, grad = pl.pallas_call(
        functools.partial(student_kernel, tokens_all=tokens_all),
        out_shape=(
            jax.ShapeDtypeStruct((half, WIDE), jnp.float32),
            jax.ShapeDtypeStruct((1, WIDE), jnp.float32),
        ),
        in_specs=[smem] + [vmem] * 5,
        out_specs=(vmem, vmem),
        scratch_shapes=[
            pltpu.VMEM((STEPS, half, WIDE), jnp.float32),
            pltpu.VMEM((half, WIDE), jnp.float32),
        ],
        compiler_params=pltpu.CompilerParams(vmem_limit_bytes=32 * 1024 * 1024),
        cost_estimate=pl.CostEstimate(
            flops=2 * 9 * half * deep * WIDE, bytes_accessed=8 * 1024 * 1024, transcendentals=18 * half * WIDE
        ),
        name="student",
    )(core[None], driven, mine_f, mine, theirs, own_threshold)

    grads = lax.all_to_all(
        jnp.broadcast_to(grad, (Y * CORE * Z * X, WIDE)), ("y", "core", "z", "x"), 0, 0, tiled=True
    )

    quarter = half // 2
    r_p, r_m = around(rates, "y", 1), around(rates, "y", -1)
    r_f = jnp.concatenate([around(r_p[:quarter], "y", 1), around(r_m[quarter:], "y", -1)])
    pieces = []
    for piece in (rates, r_m, r_f, r_p):
        pieces += [piece, other_core(piece)]
    rates_out = pl.pallas_call(
        place_kernel,
        out_shape=jax.ShapeDtypeStruct((rows, width), jnp.float32),
        in_specs=[smem] + [vmem] * 8,
        out_specs=vmem,
        name="place",
    )(jnp.stack([core, y]), *pieces)

    sums = jnp.sum(grads.reshape(Y, CORE * Z * X, WIDE), axis=1)
    grad_out = jnp.concatenate([sums[0], sums[1, 128:], sums[2], sums[3, 128:]])
    return rates_out, grad_out


def solution(mesh):
    grid = mesh.devices.reshape(Y, CORE, mesh.shape["mp"], Z, X)
    fine = Mesh(grid, ("y", "core", "mp", "z", "x"))
    tm, tok = ("y", "core"), ("z", "x")
    return jax.shard_map(
        on_device,
        mesh=fine,
        in_specs=(P(tok, None), P(tm, tok, None), P(tm + tok, "mp"), P("mp")),
        out_specs=(P(tok, "mp"), P("mp")),
        check_vma=False,
    )
```

```python
import functools
import jax
import jax.numpy as jnp
from jax import lax
from jax.experimental import pallas as pl
from jax.experimental.pallas import tpu as pltpu
from jax.sharding import Mesh, PartitionSpec as P

SHARP = 2.0
STARTS = (0, 384, 896, 1280)
WIDE = 512
Y, CORE, Z, X = 4, 2, 2, 4
STEPS = Y * CORE
MIB = 1024 * 1024


def around(x, axis, by):
    n = lax.axis_size(axis)
    return lax.ppermute(x, axis, [(i, (i + by) % n) for i in range(n)])


def across(x, by):
    pairs = [(y * CORE + c, (y + by) % Y * CORE + 1 - c) for y in range(Y) for c in range(CORE)]
    return lax.ppermute(x, ("y", "core"), pairs)


def start_of(y):
    return pl.multiple_of(jnp.where(y < 2, 0, 896) + jnp.where(y % 2 == 1, 384, 0), 128)


def prepare_kernel(mask_ref, features_ref, weight_ref, keep_ref, give_ref, payload_ref):
    half = keep_ref.shape[0]
    core = lax.axis_index("core")
    for out_ref, which in ((keep_ref, core), (give_ref, 1 - core)):
        at = pl.ds(pl.multiple_of(which * half, half), half)
        kept = jnp.where(mask_ref[0, at, :] > 0, features_ref[at, :].astype(jnp.float32), 0.0)
        out_ref[...] = kept.astype(out_ref.dtype)
    for y, s in enumerate(STARTS):
        for z in range(Z):
            payload_ref[y * Z + z] = weight_ref[:, s : s + WIDE]


def student_kernel(*refs, tokens_all):
    pieces, (features_ref, weight_ref, threshold_ref, rates_ref, grad_ref, current_ref) = refs[:STEPS], refs[STEPS:]
    half = pieces[0].shape[0]
    core, y = lax.axis_index("core"), lax.axis_index("y")
    own = pl.ds(pl.multiple_of(core * half, half), half)
    left = jnp.concatenate([p[...] for p in pieces] + [features_ref[own, :]], axis=0)
    steps = [(y + dy) % Y * CORE + (core + dc) % CORE for dy, dc in ((0, 0), (0, 1), (3, 0), (3, 1), (1, 0), (1, 1), (2, 0), (2, 1))]
    for n in range(0, WIDE, 256):
        total = jnp.dot(left, weight_ref[:, n : n + 256], preferred_element_type=jnp.float32)
        for j, step in enumerate(steps + [STEPS]):
            current_ref[step, :, n : n + 256] = total[j * half : (j + 1) * half]
    threshold = threshold_ref[:, pl.ds(start_of(y), WIDE)]
    tall = 32

    def strip(i, grad_sum):
        at = pl.ds(pl.multiple_of(i * tall, tall), tall)
        potential = jnp.zeros((tall, WIDE), jnp.float32)
        total = jnp.zeros((tall, WIDE), jnp.float32)
        for t in range(STEPS):
            rising = potential + 2.0 * current_ref[t, at, :]
            fired = jax.nn.sigmoid(SHARP * (rising - threshold))
            potential = rising - threshold * fired
            current_ref[t, at, :] = fired
            total = total + fired
        rates = threshold * total / STEPS
        rates_ref[at, :] = rates
        v = current_ref[STEPS, at, :]
        error = (rates - v * jax.nn.sigmoid(v)) / tokens_all
        cotangent = jnp.zeros((tall, WIDE), jnp.float32)
        for t in reversed(range(STEPS)):
            fired = current_ref[t, at, :]
            dspike = error * threshold / STEPS - threshold * cotangent
            dwide = dspike * SHARP * fired * (1.0 - fired)
            grad_sum = grad_sum + (-dwide - fired * cotangent + error * fired / STEPS)
            cotangent = cotangent + dwide
        return grad_sum

    grad_sum = lax.fori_loop(0, half // tall, strip, jnp.zeros((tall, WIDE), jnp.float32))
    grad_ref[...] = jnp.broadcast_to(jnp.sum(grad_sum, axis=0, keepdims=True)[None], grad_ref.shape)


def place_kernel(*refs):
    out_ref = refs[-1]
    half = out_ref.shape[0] // 2
    core, y = lax.axis_index("core"), lax.axis_index("y")
    for j in range(Y):
        source = (y + j) % Y
        start = start_of(source)
        for k in range(CORE):
            row = pl.multiple_of(((core + k) % CORE) * half, half)
            piece = refs[CORE * j + k]

            @pl.when(source % 2 == 0)
            def _():
                out_ref[pl.ds(row, half), pl.ds(start, WIDE)] = piece[...]

            @pl.when(source % 2 == 1)
            def _():
                out_ref[pl.ds(row, half), pl.ds(pl.multiple_of(start + 128, 128), WIDE - 128)] = piece[:, 128:]


def add_kernel(grads_ref, out_ref):
    count = grads_ref.shape[0] // Y
    for y, s in enumerate(STARTS):
        total = jnp.sum(grads_ref[y * count : (y + 1) * count], axis=0)
        skip = 128 * (y % 2)
        out_ref[s + skip : s + WIDE] = total[0, skip:]


def on_device(features, spike_mask, gate_weight, threshold):
    core, x = lax.axis_index("core"), lax.axis_index("x")
    rows, deep = features.shape
    tokens_all = rows * Z * X
    half = rows // CORE
    part, width = gate_weight.shape
    vmem = pl.BlockSpec(memory_space=pltpu.VMEM)

    keep, give, payload = pl.pallas_call(
        prepare_kernel,
        out_shape=(
            jax.ShapeDtypeStruct((half, deep), features.dtype),
            jax.ShapeDtypeStruct((half, deep), features.dtype),
            jax.ShapeDtypeStruct((Y * Z, part, WIDE), gate_weight.dtype),
        ),
        in_specs=[vmem] * 3,
        out_specs=(vmem,) * 3,
        compiler_params=pltpu.CompilerParams(vmem_limit_bytes=8 * MIB),
        name="prepare",
    )(spike_mask, features, gate_weight)

    together = lax.optimization_barrier
    keep_p, keep_m = around(keep, "y", 1), around(keep, "y", -1)
    got = across(give, 0)
    landed = lax.all_to_all(payload, ("y", "z"), 0, 0, tiled=True).reshape(Y, Z, part, WIDE)
    keep_p, keep_m, got, give, landed = together((keep_p, keep_m, got, give, landed))

    got_p, got_m = across(give, 1), across(give, -1)
    w_p, w_m = around(landed, "x", 1), around(landed, "x", -1)
    landed_o = around(landed, "core", 1)
    keep_p, got_p, got_m, w_p, w_m, landed_o = together((keep_p, got_p, got_m, w_p, w_m, landed_o))

    keep_f = around(keep_p, "y", 1)
    got_f = around(got_m, "y", -1)
    w_f0, w_f1 = around(w_p[: Y // 2], "x", 1), around(w_m[Y // 2 :], "x", -1)
    weight = jnp.zeros((Y, CORE, Z, X, part, WIDE), gate_weight.dtype)
    for piece, other, at_y, dx in (
        (landed, landed_o, 0, 0),
        (w_p, around(w_p, "core", 1), 0, 3),
        (w_m, around(w_m, "core", 1), 0, 1),
        (w_f0, around(w_f0, "core", 1), 0, 2),
        (w_f1, around(w_f1, "core", 1), Y // 2, 2),
    ):
        at_x = lax.rem(x + dx, X)
        for v, at_core in ((piece, core), (other, 1 - core)):
            weight = lax.dynamic_update_slice(weight, v[:, None, :, None], (at_y, at_core, 0, at_x, 0, 0))
    weight = weight.reshape(deep, WIDE)

    peers = Y * CORE * Z * X
    rates, grad = pl.pallas_call(
        functools.partial(student_kernel, tokens_all=tokens_all),
        out_shape=(
            jax.ShapeDtypeStruct((half, WIDE), jnp.float32),
            jax.ShapeDtypeStruct((peers, 1, WIDE), jnp.float32),
        ),
        in_specs=[vmem] * (STEPS + 3),
        out_specs=(vmem, vmem),
        scratch_shapes=[pltpu.VMEM((STEPS + 1, half, WIDE), jnp.float32)],
        compiler_params=pltpu.CompilerParams(vmem_limit_bytes=16 * MIB),
        cost_estimate=pl.CostEstimate(
            flops=2 * 9 * half * deep * WIDE, bytes_accessed=8 * MIB, transcendentals=18 * half * WIDE
        ),
        name="student",
    )(keep, got, keep_p, got_p, keep_m, got_m, keep_f, got_f, features, weight, threshold[None])

    grads = lax.all_to_all(grad, ("y", "core", "z", "x"), 0, 0, tiled=True)

    pieces = []
    for piece in (rates, around(rates, "y", -1), around(rates, "y", 2), around(rates, "y", 1)):
        pieces += [piece, around(piece, "core", 1)]
    rates_out = pl.pallas_call(
        place_kernel,
        out_shape=jax.ShapeDtypeStruct((rows, width), jnp.float32),
        in_specs=[vmem] * 8,
        out_specs=vmem,
        compiler_params=pltpu.CompilerParams(vmem_limit_bytes=4 * MIB),
        name="place",
    )(*pieces)
    rates_out, grads = lax.optimization_barrier((rates_out, grads))

    grad_out = pl.pallas_call(
        add_kernel,
        out_shape=jax.ShapeDtypeStruct((width,), jnp.float32),
        in_specs=[vmem],
        out_specs=vmem,
        compiler_params=pltpu.CompilerParams(vmem_limit_bytes=4 * MIB),
        name="add",
    )(grads)
    return rates_out, grad_out


def solution(mesh):
    grid = mesh.devices.reshape(Y, CORE, mesh.shape["mp"], Z, X)
    fine = Mesh(grid, ("y", "core", "mp", "z", "x"))
    tm, tok = ("y", "core"), ("z", "x")
    return jax.shard_map(
        on_device,
        mesh=fine,
        in_specs=(P(tok, None), P(tm, tok, None), P(tm + tok, "mp"), P("mp")),
        out_specs=(P(tok, "mp"), P("mp")),
        check_vma=False,
    )
```

```python
import functools
import jax
import jax.numpy as jnp
from jax import lax
from jax.experimental import pallas as pl
from jax.experimental.pallas import tpu as pltpu
from jax.sharding import Mesh, PartitionSpec as P

SHARP = 2.0
STARTS = (0, 128, 384, 640, 896, 1024, 1280, 1536)
WIDE = 256
Y, CORE, Z, X = 4, 2, 2, 4
STEPS = Y * CORE
MIB = 1024 * 1024


def around(x, axis, by):
    n = lax.axis_size(axis)
    return lax.ppermute(x, axis, [(i, (i + by) % n) for i in range(n)])


def start_of(y, core):
    w = y * CORE + core
    start = 128 * ((7 * w) // 4)
    return pl.multiple_of(start, 128)


def prepare_kernel(mask_hbm, features_hbm, weight_hbm, driven_ref, payload_ref, mask_ref, features_ref, weight_ref, sems):
    copies = [
        pltpu.make_async_copy(a, b, sems.at[i])
        for i, (a, b) in enumerate(((mask_hbm, mask_ref), (features_hbm, features_ref), (weight_hbm, weight_ref)))
    ]
    for c in copies:
        c.start()
    for c in copies[:2]:
        c.wait()
    kept = jnp.where(mask_ref[0] > 0, features_ref[...].astype(jnp.float32), 0.0)
    driven_ref[...] = kept.astype(driven_ref.dtype)
    copies[2].wait()
    for w, s in enumerate(STARTS):
        for z in range(Z):
            payload_ref[w * Z + z] = weight_ref[:, s : s + WIDE]


def student_kernel(*refs, tokens_all, spans):
    count = len(spans)
    pieces, (features_ref, weight_ref, threshold_ref, rates_ref, grad_ref, current_ref) = refs[:count], refs[count:]
    rows = features_ref.shape[0]
    core, y = lax.axis_index("core"), lax.axis_index("y")
    left = jnp.concatenate([p[...] for p in pieces] + [features_ref[...]], axis=0)
    total = jnp.dot(left, weight_ref[...], preferred_element_type=jnp.float32)
    at = 0
    for dy, dc, first, tall in spans:
        step = (y + dy) % Y * CORE + (core + dc) % CORE
        current_ref[step, first : first + tall, :] = total[at : at + tall]
        at += tall
    current_ref[STEPS] = total[at:]
    threshold = threshold_ref[:, pl.ds(start_of(y, core), WIDE)]
    tall = 64

    def strip(i, grad_sum):
        at = pl.ds(pl.multiple_of(i * tall, tall), tall)
        potential = jnp.zeros((tall, WIDE), jnp.float32)
        total = jnp.zeros((tall, WIDE), jnp.float32)
        for t in range(STEPS):
            rising = potential + 2.0 * current_ref[t, at, :]
            fired = jax.nn.sigmoid(SHARP * (rising - threshold))
            potential = rising - threshold * fired
            current_ref[t, at, :] = fired
            total = total + fired
        rates = threshold * total / STEPS
        rates_ref[at, :] = rates
        v = current_ref[STEPS, at, :]
        error = (rates - v * jax.nn.sigmoid(v)) / tokens_all
        cotangent = jnp.zeros((tall, WIDE), jnp.float32)
        for t in reversed(range(STEPS)):
            fired = current_ref[t, at, :]
            dspike = error * threshold / STEPS - threshold * cotangent
            dwide = dspike * SHARP * fired * (1.0 - fired)
            grad_sum = grad_sum + (-dwide - fired * cotangent + error * fired / STEPS)
            cotangent = cotangent + dwide
        return grad_sum

    grad_sum = lax.fori_loop(0, rows // tall, strip, jnp.zeros((tall, WIDE), jnp.float32))
    grad_ref[...] = jnp.broadcast_to(jnp.sum(grad_sum, axis=0, keepdims=True)[None], grad_ref.shape)


def place_kernel(*refs):
    out_ref = refs[-1]
    core, y = lax.axis_index("core"), lax.axis_index("y")
    for j in range(Y):
        for k in range(CORE):
            from_y, from_core = (y + j) % Y, (core + k) % CORE
            start = start_of(from_y, from_core)
            piece = refs[CORE * j + k]

            @pl.when((from_core == 0) | (from_y % 2 == 1))
            def _():
                out_ref[:, pl.ds(start, WIDE)] = piece[...]

            @pl.when((from_core == 1) & (from_y % 2 == 0))
            def _():
                out_ref[:, pl.ds(pl.multiple_of(start + 128, 128), WIDE - 128)] = piece[:, 128:]


def add_kernel(grads_ref, out_ref):
    count = grads_ref.shape[0] // STEPS
    for w, s in enumerate(STARTS):
        total = jnp.sum(grads_ref[w * count : (w + 1) * count], axis=0)
        skip = 128 if w % 4 == 1 else 0
        out_ref[s + skip : s + WIDE] = total[0, skip:]


def on_device(features, spike_mask, gate_weight, threshold):
    x = lax.axis_index("x")
    rows, deep = features.shape
    tokens_all = rows * Z * X
    half = rows // 2
    part, width = gate_weight.shape
    vmem = pl.BlockSpec(memory_space=pltpu.VMEM)

    own, payload = pl.pallas_call(
        prepare_kernel,
        out_shape=(
            jax.ShapeDtypeStruct((rows, deep), features.dtype),
            jax.ShapeDtypeStruct((STEPS * Z, part, WIDE), gate_weight.dtype),
        ),
        in_specs=[pl.BlockSpec(memory_space=pltpu.HBM)] * 3,
        out_specs=(vmem,) * 2,
        scratch_shapes=[
            pltpu.VMEM(spike_mask.shape, spike_mask.dtype),
            pltpu.VMEM(features.shape, features.dtype),
            pltpu.VMEM(gate_weight.shape, gate_weight.dtype),
            pltpu.SemaphoreType.DMA((3,)),
        ],
        compiler_params=pltpu.CompilerParams(vmem_limit_bytes=8 * MIB),
        name="prepare",
    )(spike_mask, features, gate_weight)

    s_p, s_m = around(own, "y", 1), around(own, "y", -1)
    s_f0, s_f1 = around(s_p[:half], "y", 1), around(s_m[half:], "y", -1)

    landed = lax.all_to_all(payload, ("y", "core", "z"), 0, 0, tiled=True).reshape(STEPS, Z, part, WIDE)
    w_p, w_m = around(landed, "x", 1), around(landed, "x", -1)
    cut = STEPS // 2
    w_f0, w_f1 = around(w_p[:cut], "x", 1), around(w_m[cut:], "x", -1)
    s_q, s_n, w_f0, w_f1 = lax.optimization_barrier((s_p, s_m, w_f0, w_f1))
    o_own, o_p, o_m = (around(v, "core", 1) for v in (own, s_q, s_n))
    o_f0, o_f1 = around(s_f0, "core", 1), around(s_f1, "core", 1)
    steps, spans = [], []
    for mine, other, dy, first, tall in (
        (own, o_own, 0, 0, rows), (s_p, o_p, 3, 0, rows), (s_m, o_m, 1, 0, rows), (s_f0, o_f0, 2, 0, half), (s_f1, o_f1, 2, half, half),
    ):
        steps += [mine, other]
        spans += [(dy, 0, first, tall), (dy, 1, first, tall)]

    weight = jnp.zeros((STEPS, Z, X, part, WIDE), gate_weight.dtype)
    for piece, at, dx in ((landed, 0, 0), (w_p, 0, 3), (w_m, 0, 1), (w_f0, 0, 2), (w_f1, cut, 2)):
        weight = lax.dynamic_update_slice(weight, piece[:, :, None], (at, 0, lax.rem(x + dx, X), 0, 0))
    weight = weight.reshape(deep, WIDE)

    peers = Y * CORE * Z * X
    rates, grad = pl.pallas_call(
        functools.partial(student_kernel, tokens_all=tokens_all, spans=spans),
        out_shape=(
            jax.ShapeDtypeStruct((rows, WIDE), jnp.float32),
            jax.ShapeDtypeStruct((peers, 1, WIDE), jnp.float32),
        ),
        in_specs=[vmem] * (len(steps) + 3),
        out_specs=(vmem, vmem),
        scratch_shapes=[pltpu.VMEM((STEPS + 1, rows, WIDE), jnp.float32)],
        compiler_params=pltpu.CompilerParams(vmem_limit_bytes=12 * MIB),
        cost_estimate=pl.CostEstimate(
            flops=2 * 9 * rows * deep * WIDE, bytes_accessed=8 * MIB, transcendentals=18 * rows * WIDE
        ),
        name="student",
    )(*steps, features, weight, threshold[None])

    grads = lax.all_to_all(grad, ("y", "core", "z", "x"), 0, 0, tiled=True)

    pieces = []
    for piece in (rates, around(rates, "y", -1), around(rates, "y", 2), around(rates, "y", 1)):
        pieces += [piece, around(piece, "core", 1)]
    rates_out = pl.pallas_call(
        place_kernel,
        out_shape=jax.ShapeDtypeStruct((rows, width), jnp.float32),
        in_specs=[vmem] * 8,
        out_specs=vmem,
        compiler_params=pltpu.CompilerParams(vmem_limit_bytes=4 * MIB),
        cost_estimate=pl.CostEstimate(flops=0, bytes_accessed=0, transcendentals=0),
        name="place",
    )(*pieces)
    rates_out, grads = lax.optimization_barrier((rates_out, grads))

    grad_out = pl.pallas_call(
        add_kernel,
        out_shape=jax.ShapeDtypeStruct((width,), jnp.float32),
        in_specs=[vmem],
        out_specs=vmem,
        compiler_params=pltpu.CompilerParams(vmem_limit_bytes=4 * MIB),
        cost_estimate=pl.CostEstimate(flops=0, bytes_accessed=64 * MIB, transcendentals=0),
        name="add",
    )(grads)
    return rates_out, grad_out


def solution(mesh):
    grid = mesh.devices.reshape(Y, CORE, mesh.shape["mp"], Z, X)
    fine = Mesh(grid, ("y", "core", "mp", "z", "x"))
    tm, tok = ("y", "core"), ("z", "x")
    return jax.shard_map(
        on_device,
        mesh=fine,
        in_specs=(P(tok, None), P(tm, tok, None), P(tm + tok, "mp"), P("mp")),
        out_specs=(P(tok, "mp"), P("mp")),
        check_vma=False,
    )
```

```python
import functools
import jax
import jax.numpy as jnp
from jax import lax
from jax.experimental import pallas as pl
from jax.experimental.pallas import tpu as pltpu
from jax.sharding import Mesh, PartitionSpec as P

SHARP = 2.0
STARTS = (0, 128, 384, 640, 896, 1024, 1280, 1536)
WIDE = 256
Y, CORE, Z, X = 4, 2, 2, 4
STEPS = Y * CORE
MIB = 1024 * 1024


def around(x, axis, by):
    n = lax.axis_size(axis)
    return lax.ppermute(x, axis, [(i, (i + by) % n) for i in range(n)])


def start_of(y, core):
    w = y * CORE + core
    start = 128 * ((7 * w) // 4)
    return pl.multiple_of(start, 128)


def window_kernel(weight_ref, payload_ref):
    for w, s in enumerate(STARTS):
        payload_ref[w] = weight_ref[:, s : s + WIDE]


def assemble_kernel(*refs):
    pieces, out_ref = refs[:-1], refs[-1]
    z, x = lax.axis_index("z"), lax.axis_index("x")
    for i, piece in enumerate(pieces):
        out_ref[:, (z + i // X) % Z, (x + i % X) % X] = piece[...]


def drive_kernel(mask_hbm, features_hbm, driven_hbm, mask_ref, features_ref, driven_ref, sems):
    parts = sems.shape[0]
    tall = features_ref.shape[0] // parts
    spans = [pl.ds(i * tall, tall) for i in range(parts)]
    arriving = [
        (
            pltpu.make_async_copy(mask_hbm.at[0, at], mask_ref.at[at], sems.at[i, 0]),
            pltpu.make_async_copy(features_hbm.at[at], features_ref.at[at], sems.at[i, 1]),
        )
        for i, at in enumerate(spans)
    ]
    leaving = [pltpu.make_async_copy(driven_ref.at[at], driven_hbm.at[at], sems.at[i, 2]) for i, at in enumerate(spans)]
    for pair in arriving:
        for copy in pair:
            copy.start()
    for at, pair, out in zip(spans, arriving, leaving):
        for copy in pair:
            copy.wait()
        kept = jnp.where(mask_ref[at, :] > 0, features_ref[at, :].astype(jnp.float32), 0.0)
        driven_ref[at, :] = kept.astype(driven_ref.dtype)
        out.start()
    for out in leaving:
        out.wait()


def student_kernel(*refs, tokens_all, spans):
    count = len(spans)
    pieces, (features_ref, weight_ref, threshold_ref, rates_ref, grad_ref, current_ref) = refs[:count], refs[count:]
    rows = features_ref.shape[0]
    core, y = lax.axis_index("core"), lax.axis_index("y")
    left = jnp.concatenate([p[...] for p in pieces] + [features_ref[...]], axis=0)
    total = jnp.dot(left, weight_ref[...], preferred_element_type=jnp.float32)
    at = 0
    for dy, dc, first, tall in spans:
        step = (y + dy) % Y * CORE + (core + dc) % CORE
        current_ref[step, first : first + tall, :] = total[at : at + tall]
        at += tall
    current_ref[STEPS] = total[at:]
    threshold = threshold_ref[:, pl.ds(start_of(y, core), WIDE)]
    tall = 64

    def strip(i, grad_sum):
        at = pl.ds(pl.multiple_of(i * tall, tall), tall)
        potential = jnp.zeros((tall, WIDE), jnp.float32)
        total = jnp.zeros((tall, WIDE), jnp.float32)
        for t in range(STEPS):
            rising = potential + 2.0 * current_ref[t, at, :]
            fired = jax.nn.sigmoid(SHARP * (rising - threshold))
            potential = rising - threshold * fired
            current_ref[t, at, :] = fired
            total = total + fired
        rates = threshold * total / STEPS
        rates_ref[at, :] = rates
        v = current_ref[STEPS, at, :]
        error = (rates - v * jax.nn.sigmoid(v)) / tokens_all
        cotangent = jnp.zeros((tall, WIDE), jnp.float32)
        for t in reversed(range(STEPS)):
            fired = current_ref[t, at, :]
            dspike = error * threshold / STEPS - threshold * cotangent
            dwide = dspike * SHARP * fired * (1.0 - fired)
            grad_sum = grad_sum + (-dwide - fired * cotangent + error * fired / STEPS)
            cotangent = cotangent + dwide
        return grad_sum

    grad_sum = lax.fori_loop(0, rows // tall, strip, jnp.zeros((tall, WIDE), jnp.float32))
    grad_ref[...] = jnp.broadcast_to(jnp.sum(grad_sum, axis=0, keepdims=True)[None], grad_ref.shape)


def place_kernel(mine_ref, other_ref, out_ref):
    rows = out_ref.shape[0]
    core, y = lax.axis_index("core"), lax.axis_index("y")
    for j in range(Y):
        for k, piece in enumerate((mine_ref, other_ref)):
            from_y, from_core = (y + j) % Y, (core + k) % CORE
            start = start_of(from_y, from_core)
            at = slice(j * rows, (j + 1) * rows)

            @pl.when((from_core == 0) | (from_y % 2 == 1))
            def _():
                out_ref[:, pl.ds(start, WIDE)] = piece[at, :]

            @pl.when((from_core == 1) & (from_y % 2 == 0))
            def _():
                out_ref[:, pl.ds(pl.multiple_of(start + 128, 128), WIDE - 128)] = piece[at, 128:]


def add_kernel(grads_ref, out_ref):
    count = grads_ref.shape[0] // STEPS
    for w, s in enumerate(STARTS):
        total = jnp.sum(grads_ref[w * count : (w + 1) * count], axis=0)
        skip = 128 if w % 4 == 1 else 0
        out_ref[s + skip : s + WIDE] = total[0, skip:]


def on_device(features, spike_mask, gate_weight, threshold):
    rows, deep = features.shape
    tokens_all = rows * Z * X
    half = rows // 2
    part, width = gate_weight.shape
    vmem = pl.BlockSpec(memory_space=pltpu.VMEM)

    def along_x(held):
        return around(held, "x", -1), around(held, "x", 2), around(held, "x", 1)

    hbm = pl.BlockSpec(memory_space=pl.ANY)
    own = pl.pallas_call(
        drive_kernel,
        out_shape=jax.ShapeDtypeStruct((rows, deep), features.dtype),
        in_specs=[hbm] * 2,
        out_specs=hbm,
        scratch_shapes=[
            pltpu.VMEM((rows, deep), spike_mask.dtype),
            pltpu.VMEM((rows, deep), features.dtype),
            pltpu.VMEM((rows, deep), features.dtype),
            pltpu.SemaphoreType.DMA((4, 3)),
        ],
        compiler_params=pltpu.CompilerParams(vmem_limit_bytes=60 * MIB),
        name="drive",
    )(spike_mask, features)

    payload = pl.pallas_call(
        window_kernel,
        out_shape=jax.ShapeDtypeStruct((STEPS, part, WIDE), gate_weight.dtype),
        in_specs=[vmem],
        out_specs=vmem,
        compiler_params=pltpu.CompilerParams(vmem_limit_bytes=4 * MIB),
        name="windows",
    )(gate_weight)
    near_w = lax.all_to_all(payload, ("y", "core"), 0, 0, tiled=True)
    own, near_w = lax.optimization_barrier((own, near_w))
    s_p, s_m = around(own, "y", 1), around(own, "y", -1)
    near_x = along_x(near_w)
    far_w = around(near_w, "z", 1)
    s_p, s_m, far_w, *near_x = lax.optimization_barrier((s_p, s_m, far_w, *near_x))
    s_f0, s_f1 = around(s_p[:half], "y", 1), around(s_m[half:], "y", -1)
    far_x = along_x(far_w)
    s_f0, s_f1, *far_x = lax.optimization_barrier((s_f0, s_f1, *far_x))
    o_own, o_p, o_m = (around(v, "core", 1) for v in (own, s_p, s_m))
    o_f0, o_f1 = around(s_f0, "core", 1), around(s_f1, "core", 1)
    steps, spans = [], []
    for mine, other, dy, first, tall in (
        (own, o_own, 0, 0, rows), (s_p, o_p, 3, 0, rows), (s_m, o_m, 1, 0, rows), (s_f0, o_f0, 2, 0, half), (s_f1, o_f1, 2, half, half),
    ):
        steps += [mine, other]
        spans += [(dy, 0, first, tall), (dy, 1, first, tall)]
    weight = pl.pallas_call(
        assemble_kernel,
        out_shape=jax.ShapeDtypeStruct((STEPS, Z, X, part, WIDE), gate_weight.dtype),
        in_specs=[vmem] * (Z * X),
        out_specs=vmem,
        compiler_params=pltpu.CompilerParams(vmem_limit_bytes=8 * MIB),
        name="assemble",
    )(near_w, *near_x, far_w, *far_x)
    weight = weight.reshape(deep, WIDE)

    peers = STEPS * Z * X
    rates, grad = pl.pallas_call(
        functools.partial(student_kernel, tokens_all=tokens_all, spans=spans),
        out_shape=(
            jax.ShapeDtypeStruct((rows, WIDE), jnp.float32),
            jax.ShapeDtypeStruct((peers, 1, WIDE), jnp.float32),
        ),
        in_specs=[vmem] * (len(steps) + 3),
        out_specs=(vmem, vmem),
        scratch_shapes=[pltpu.VMEM((STEPS + 1, rows, WIDE), jnp.float32)],
        compiler_params=pltpu.CompilerParams(vmem_limit_bytes=12 * MIB),
        cost_estimate=pl.CostEstimate(
            flops=2 * 9 * rows * deep * WIDE, bytes_accessed=8 * MIB, transcendentals=18 * rows * WIDE
        ),
        name="student",
    )(*steps, features, weight, threshold[None])

    rates_y = [around(rates, "y", -1), around(rates, "y", 2), around(rates, "y", 1)]
    grads = lax.all_to_all(grad, ("y", "core", "z", "x"), 0, 0, tiled=True)
    *rates_y, grads = lax.optimization_barrier((*rates_y, grads))
    mine = jnp.concatenate([rates] + rates_y)
    other = around(mine, "core", 1)
    rates_out = pl.pallas_call(
        place_kernel,
        out_shape=jax.ShapeDtypeStruct((rows, width), jnp.float32),
        in_specs=[vmem] * 2,
        out_specs=vmem,
        compiler_params=pltpu.CompilerParams(vmem_limit_bytes=4 * MIB),
        cost_estimate=pl.CostEstimate(flops=0, bytes_accessed=0, transcendentals=0),
        name="place",
    )(mine, other)


    grad_out = pl.pallas_call(
        add_kernel,
        out_shape=jax.ShapeDtypeStruct((width,), jnp.float32),
        in_specs=[vmem],
        out_specs=vmem,
        compiler_params=pltpu.CompilerParams(vmem_limit_bytes=4 * MIB),
        name="add",
    )(grads)
    return rates_out, grad_out


def solution(mesh):
    grid = mesh.devices.reshape(Y, CORE, mesh.shape["mp"], Z, X)
    fine = Mesh(grid, ("y", "core", "mp", "z", "x"))
    tm, tok = ("y", "core"), ("z", "x")
    return jax.shard_map(
        on_device,
        mesh=fine,
        in_specs=(P(tok, None), P(tm, tok, None), P(tm + tok, "mp"), P("mp")),
        out_specs=(P(tok, "mp"), P("mp")),
        check_vma=False,
    )
```

```python
import functools
import jax
import jax.numpy as jnp
from jax import lax
from jax.experimental import pallas as pl
from jax.experimental.pallas import tpu as pltpu
from jax.sharding import Mesh, PartitionSpec as P

SHARP = 2.0
STARTS = (0, 128, 384, 640, 896, 1024, 1280, 1536)
WIDE = 256
Y, CORE, Z, X = 4, 2, 2, 4
STEPS = Y * CORE
MIB = 1024 * 1024
GROUPS = ((0, 24), (24, 48), (48, 64))


def around(x, axis, by):
    n = lax.axis_size(axis)
    return lax.ppermute(x, axis, [(i, (i + by) % n) for i in range(n)])


def start_of(y, core):
    w = y * CORE + core
    start = 128 * ((7 * w) // 4)
    return pl.multiple_of(start, 128)


def window_kernel(weight_ref, payload_ref):
    for w, s in enumerate(STARTS):
        payload_ref[w] = weight_ref[:, s : s + WIDE]


def assemble_kernel(*refs):
    pieces, out_ref = refs[:-1], refs[-1]
    z, x = lax.axis_index("z"), lax.axis_index("x")
    for i, piece in enumerate(pieces):
        out_ref[:, (z + i // X) % Z, (x + i % X) % X] = piece[...]


def drive_kernel(mask_hbm, features_hbm, driven_hbm, mask_ref, features_ref, driven_ref, sems):
    parts = sems.shape[0]
    tall = features_ref.shape[0] // parts
    spans = [pl.ds(i * tall, tall) for i in range(parts)]
    arriving = [
        (
            pltpu.make_async_copy(mask_hbm.at[0, at], mask_ref.at[at], sems.at[i, 0]),
            pltpu.make_async_copy(features_hbm.at[at], features_ref.at[at], sems.at[i, 1]),
        )
        for i, at in enumerate(spans)
    ]
    leaving = [pltpu.make_async_copy(driven_ref.at[at], driven_hbm.at[at], sems.at[i, 2]) for i, at in enumerate(spans)]
    for pair in arriving:
        for copy in pair:
            copy.start()
    for at, pair, out in zip(spans, arriving, leaving):
        for copy in pair:
            copy.wait()
        kept = jnp.where(mask_ref[at, :] > 0, features_ref[at, :].astype(jnp.float32), 0.0)
        driven_ref[at, :] = kept.astype(driven_ref.dtype)
        out.start()
    for out in leaving:
        out.wait()


def student_kernel(*refs, tokens_all, spans):
    count = len(spans)
    pieces, (features_ref, weight_ref, threshold_ref, rates_ref, grad_ref, current_ref) = refs[:count], refs[count:]
    rows = features_ref.shape[0]
    core, y = lax.axis_index("core"), lax.axis_index("y")
    left = jnp.concatenate([p[...] for p in pieces] + [features_ref[...]], axis=0)
    total = jnp.dot(left, weight_ref[...], preferred_element_type=jnp.float32)
    at = 0
    for dy, dc, first, tall in spans:
        step = (y + dy) % Y * CORE + (core + dc) % CORE
        current_ref[step, first : first + tall, :] = total[at : at + tall]
        at += tall
    current_ref[STEPS] = total[at:]
    threshold = threshold_ref[:, pl.ds(start_of(y, core), WIDE)]
    tall = GROUPS[-1][1]

    def strip(i, grad_sum):
        at = pl.ds(pl.multiple_of(i * tall, tall), tall)
        potential = jnp.zeros((tall, WIDE), jnp.float32)
        total = jnp.zeros((tall, WIDE), jnp.float32)
        for t in range(STEPS):
            rising = potential + 2.0 * current_ref[t, at, :]
            fired = jax.nn.sigmoid(SHARP * (rising - threshold))
            potential = rising - threshold * fired
            current_ref[t, at, :] = fired
            total = total + fired
        rates = threshold * total / STEPS
        rates_ref[at, :] = rates
        v = current_ref[STEPS, at, :]
        error = (rates - v * jax.nn.sigmoid(v)) / tokens_all
        cotangent = jnp.zeros((tall, WIDE), jnp.float32)
        for t in reversed(range(STEPS)):
            fired = current_ref[t, at, :]
            dspike = error * threshold / STEPS - threshold * cotangent
            dwide = dspike * SHARP * fired * (1.0 - fired)
            grad_sum = grad_sum + (-dwide - fired * cotangent + error * fired / STEPS)
            cotangent = cotangent + dwide
        return grad_sum

    grad_sum = lax.fori_loop(0, rows // tall, strip, jnp.zeros((tall, WIDE), jnp.float32))
    for i, (first, last) in enumerate(GROUPS):
        part = jnp.sum(grad_sum[first:last], axis=0, keepdims=True)
        grad_ref[:, :, i * WIDE : (i + 1) * WIDE] = jnp.broadcast_to(part[None], (grad_ref.shape[0], 1, WIDE))


def finish_kernel(*refs):
    grads_ref, rates_ref, grad_ref = refs[-3:]
    core, y = lax.axis_index("core"), lax.axis_index("y")
    for j in range(Y):
        for k in range(CORE):
            piece = refs[Y * k + j]
            from_y, from_core = (y + j) % Y, (core + k) % CORE
            start = start_of(from_y, from_core)

            @pl.when((from_core == 0) | (from_y % 2 == 1))
            def _():
                rates_ref[:, pl.ds(start, WIDE)] = piece[...]

            @pl.when((from_core == 1) & (from_y % 2 == 0))
            def _():
                rates_ref[:, pl.ds(pl.multiple_of(start + 128, 128), WIDE - 128)] = piece[:, 128:]

    count = grads_ref.shape[0] // STEPS
    for w, s in enumerate(STARTS):
        total = jnp.sum(grads_ref[w * count : (w + 1) * count], axis=0)
        total = sum(total[:, i : i + WIDE] for i in range(0, total.shape[1], WIDE))
        skip = 128 if w % 4 == 1 else 0
        grad_ref[s + skip : s + WIDE] = total[0, skip:]


def on_device(features, spike_mask, gate_weight, threshold):
    rows, deep = features.shape
    tokens_all = rows * Z * X
    half = rows // 2
    part, width = gate_weight.shape
    vmem = pl.BlockSpec(memory_space=pltpu.VMEM)

    def along_x(held):
        return around(held, "x", -1), around(held, "x", 2), around(held, "x", 1)

    hbm = pl.BlockSpec(memory_space=pl.ANY)
    own = pl.pallas_call(
        drive_kernel,
        out_shape=jax.ShapeDtypeStruct((rows, deep), features.dtype),
        in_specs=[hbm] * 2,
        out_specs=hbm,
        scratch_shapes=[
            pltpu.VMEM((rows, deep), spike_mask.dtype),
            pltpu.VMEM((rows, deep), features.dtype),
            pltpu.VMEM((rows, deep), features.dtype),
            pltpu.SemaphoreType.DMA((4, 3)),
        ],
        compiler_params=pltpu.CompilerParams(vmem_limit_bytes=60 * MIB),
        name="drive",
    )(spike_mask, features)

    payload = pl.pallas_call(
        window_kernel,
        out_shape=jax.ShapeDtypeStruct((STEPS, part, WIDE), gate_weight.dtype),
        in_specs=[vmem],
        out_specs=vmem,
        compiler_params=pltpu.CompilerParams(vmem_limit_bytes=4 * MIB),
        name="windows",
    )(gate_weight)
    near_w = lax.all_to_all(payload, ("y", "core"), 0, 0, tiled=True)
    own, near_w = lax.optimization_barrier((own, near_w))
    s_p, s_m = around(own, "y", 1), around(own, "y", -1)
    near_x = along_x(near_w)
    far_w = around(near_w, "z", 1)
    n_1, n_2, n_3 = near_x
    far_w, n_1, n_3 = lax.optimization_barrier((far_w, n_1, n_3))
    s_f0, s_f1 = around(s_p[:half], "y", 1), around(s_m[half:], "y", -1)
    far_x = along_x(far_w)
    s_f0, s_f1, n_2, *far_x = lax.optimization_barrier((s_f0, s_f1, n_2, *far_x))
    near_x = (n_1, n_2, n_3)
    o_own, o_p, o_m = (around(v, "core", 1) for v in (own, s_p, s_m))
    o_f0, o_f1 = around(s_f0, "core", 1), around(s_f1, "core", 1)
    steps, spans = [], []
    for mine, other, dy, first, tall in (
        (own, o_own, 0, 0, rows), (s_p, o_p, 3, 0, rows), (s_m, o_m, 1, 0, rows), (s_f0, o_f0, 2, 0, half), (s_f1, o_f1, 2, half, half),
    ):
        steps += [mine, other]
        spans += [(dy, 0, first, tall), (dy, 1, first, tall)]
    weight = pl.pallas_call(
        assemble_kernel,
        out_shape=jax.ShapeDtypeStruct((STEPS, Z, X, part, WIDE), gate_weight.dtype),
        in_specs=[vmem] * (Z * X),
        out_specs=vmem,
        compiler_params=pltpu.CompilerParams(vmem_limit_bytes=8 * MIB),
        name="assemble",
    )(near_w, *near_x, far_w, *far_x)
    weight = weight.reshape(deep, WIDE)

    peers = STEPS * Z * X
    rates, grad = pl.pallas_call(
        functools.partial(student_kernel, tokens_all=tokens_all, spans=spans),
        out_shape=(
            jax.ShapeDtypeStruct((rows, WIDE), jnp.float32),
            jax.ShapeDtypeStruct((peers, 1, len(GROUPS) * WIDE), jnp.float32),
        ),
        in_specs=[vmem] * (len(steps) + 3),
        out_specs=(vmem, vmem),
        scratch_shapes=[pltpu.VMEM((STEPS + 1, rows, WIDE), jnp.float32)],
        compiler_params=pltpu.CompilerParams(vmem_limit_bytes=12 * MIB),
        cost_estimate=pl.CostEstimate(
            flops=2 * 9 * rows * deep * WIDE, bytes_accessed=8 * MIB, transcendentals=18 * rows * WIDE
        ),
        name="student",
    )(*steps, features, weight, threshold[None])

    rates_y = [around(rates, "y", -1), around(rates, "y", 2), around(rates, "y", 1)]
    grads = lax.all_to_all(grad, ("y", "core", "z", "x"), 0, 0, tiled=True)
    pieces = [rates] + rates_y
    other = [around(v, "core", 1) for v in pieces]
    return pl.pallas_call(
        finish_kernel,
        out_shape=(
            jax.ShapeDtypeStruct((rows, width), jnp.float32),
            jax.ShapeDtypeStruct((width,), jnp.float32),
        ),
        in_specs=[vmem] * (2 * Y + 1),
        out_specs=(vmem, vmem),
        compiler_params=pltpu.CompilerParams(vmem_limit_bytes=6 * MIB),
        name="finish",
    )(*pieces, *other, grads)


def solution(mesh):
    grid = mesh.devices.reshape(Y, CORE, mesh.shape["mp"], Z, X)
    fine = Mesh(grid, ("y", "core", "mp", "z", "x"))
    tm, tok = ("y", "core"), ("z", "x")
    return jax.shard_map(
        on_device,
        mesh=fine,
        in_specs=(P(tok, None), P(tm, tok, None), P(tm + tok, "mp"), P("mp")),
        out_specs=(P(tok, "mp"), P("mp")),
        check_vma=False,
    )
```

```python
import functools
import jax
import jax.numpy as jnp
from jax import lax
from jax.experimental import pallas as pl
from jax.experimental.pallas import tpu as pltpu
from jax.sharding import Mesh, PartitionSpec as P

SHARP = 2.0
STARTS = (0, 128, 384, 640, 896, 1024, 1280, 1536)
WIDE = 256
Y, CORE, Z, X = 4, 2, 2, 4
STEPS = Y * CORE
MIB = 1024 * 1024
LANES = 128
GROUPS = 4


def around(x, axis, by):
    n = lax.axis_size(axis)
    return lax.ppermute(x, axis, [(i, (i + by) % n) for i in range(n)])


def start_of(y, core):
    w = y * CORE + core
    start = 128 * ((7 * w) // 4)
    return pl.multiple_of(start, 128)


def window_kernel(weight_ref, payload_ref):
    for w, s in enumerate(STARTS):
        payload_ref[w] = weight_ref[:, s : s + WIDE]


def assemble_kernel(*refs):
    pieces, out_ref = refs[:-1], refs[-1]
    z, x = lax.axis_index("z"), lax.axis_index("x")
    for i, piece in enumerate(pieces):
        out_ref[:, (z + i // X) % Z, (x + i % X) % X] = piece[...]


def drive_kernel(mask_hbm, features_hbm, driven_hbm, mask_ref, features_ref, driven_ref, sems):
    parts = sems.shape[0]
    tall = features_ref.shape[0] // parts
    spans = [pl.ds(i * tall, tall) for i in range(parts)]
    arriving = [
        (
            pltpu.make_async_copy(mask_hbm.at[0, at], mask_ref.at[at], sems.at[i, 0]),
            pltpu.make_async_copy(features_hbm.at[at], features_ref.at[at], sems.at[i, 1]),
        )
        for i, at in enumerate(spans)
    ]
    leaving = [pltpu.make_async_copy(driven_ref.at[at], driven_hbm.at[at], sems.at[i, 2]) for i, at in enumerate(spans)]
    for pair in arriving:
        for copy in pair:
            copy.start()
    for at, pair, out in zip(spans, arriving, leaving):
        for copy in pair:
            copy.wait()
        kept = jnp.where(mask_ref[at, :] > 0, features_ref[at, :].astype(jnp.float32), 0.0)
        driven_ref[at, :] = kept.astype(driven_ref.dtype)
        out.start()
    for out in leaving:
        out.wait()


def student_kernel(*refs, tokens_all, spans):
    count = len(spans)
    pieces, (features_ref, weight_ref, threshold_ref, rates_ref, grad_ref, current_ref) = refs[:count], refs[count:]
    rows = features_ref.shape[0]
    core, y = lax.axis_index("core"), lax.axis_index("y")
    cut = 4
    for part in (range(cut), range(cut, count)):
        last = part.stop == count
        held = [pieces[i][...] for i in part] + ([features_ref[...]] if last else [])
        total = jnp.dot(jnp.concatenate(held, axis=0), weight_ref[...], preferred_element_type=jnp.float32)
        at = 0
        for i in part:
            dy, dc, first, tall = spans[i]
            step = (y + dy) % Y * CORE + (core + dc) % CORE
            current_ref[step, first : first + tall, :] = total[at : at + tall]
            at += tall
        if last:
            current_ref[STEPS] = total[at:]
    threshold = threshold_ref[:, pl.ds(start_of(y, core), WIDE)]
    potential = jnp.zeros((rows, WIDE), jnp.float32)
    total = jnp.zeros((rows, WIDE), jnp.float32)
    for t in range(STEPS):
        rising = potential + 2.0 * current_ref[t]
        fired = jax.nn.sigmoid(SHARP * (rising - threshold))
        potential = rising - threshold * fired
        current_ref[t] = fired
        total = total + fired
    rates = threshold * total / STEPS
    rates_ref[...] = rates
    v = current_ref[STEPS]
    share = (rates - v * jax.nn.sigmoid(v)) / tokens_all / STEPS
    cotangent = jnp.zeros((rows, WIDE), jnp.float32)
    grad_sum = jnp.zeros((rows, WIDE), jnp.float32)
    for t in reversed(range(STEPS)):
        fired = current_ref[t]
        pull = share - cotangent
        dwide = pull * (SHARP * threshold) * (fired * (1.0 - fired))
        grad_sum = grad_sum + (fired * pull - dwide)
        cotangent = cotangent + dwide
    tall = rows // GROUPS
    parts = [jnp.sum(grad_sum[g * tall : (g + 1) * tall], axis=0, keepdims=True) for g in range(GROUPS)]
    tile = jnp.concatenate([p[:, h : h + LANES] for p in parts for h in range(0, WIDE, LANES)], axis=0)
    grad_ref[...] = jnp.broadcast_to(tile[None], grad_ref.shape)


def finish_kernel(*refs):
    grads_ref, rates_ref, grad_ref = refs[-3:]
    core, y = lax.axis_index("core"), lax.axis_index("y")
    for j in range(Y):
        for k in range(CORE):
            piece = refs[Y * k + j]
            from_y, from_core = (y + j) % Y, (core + k) % CORE
            start = start_of(from_y, from_core)

            @pl.when((from_core == 0) | (from_y % 2 == 1))
            def _():
                rates_ref[:, pl.ds(start, WIDE)] = piece[...]

            @pl.when((from_core == 1) & (from_y % 2 == 0))
            def _():
                rates_ref[:, pl.ds(pl.multiple_of(start + 128, 128), WIDE - 128)] = piece[:, 128:]

    count = grads_ref.shape[0] // STEPS
    for w, s in enumerate(STARTS):
        tile = jnp.sum(grads_ref[w * count : (w + 1) * count], axis=0)
        for h in range(WIDE // LANES):
            if w % 4 == 1 and h == 0:
                continue
            lanes = sum(tile[i : i + 1] for i in range(h, tile.shape[0], WIDE // LANES))
            grad_ref[s + h * LANES : s + (h + 1) * LANES] = lanes[0]


def on_device(features, spike_mask, gate_weight, threshold):
    rows, deep = features.shape
    tokens_all = rows * Z * X
    half = rows // 2
    part, width = gate_weight.shape
    vmem = pl.BlockSpec(memory_space=pltpu.VMEM)

    def along_x(held):
        return around(held, "x", -1), around(held, "x", 2), around(held, "x", 1)

    hbm = pl.BlockSpec(memory_space=pl.ANY)
    own = pl.pallas_call(
        drive_kernel,
        out_shape=jax.ShapeDtypeStruct((rows, deep), features.dtype),
        in_specs=[hbm] * 2,
        out_specs=hbm,
        scratch_shapes=[
            pltpu.VMEM((rows, deep), spike_mask.dtype),
            pltpu.VMEM((rows, deep), features.dtype),
            pltpu.VMEM((rows, deep), features.dtype),
            pltpu.SemaphoreType.DMA((4, 3)),
        ],
        compiler_params=pltpu.CompilerParams(vmem_limit_bytes=60 * MIB),
        name="drive",
    )(spike_mask, features)

    payload = pl.pallas_call(
        window_kernel,
        out_shape=jax.ShapeDtypeStruct((STEPS, part, WIDE), gate_weight.dtype),
        in_specs=[vmem],
        out_specs=vmem,
        compiler_params=pltpu.CompilerParams(vmem_limit_bytes=4 * MIB),
        name="windows",
    )(gate_weight)
    near_w = lax.all_to_all(payload, ("y", "core"), 0, 0, tiled=True)
    own, near_w = lax.optimization_barrier((own, near_w))
    s_p, s_m = around(own, "y", 1), around(own, "y", -1)
    near_x = along_x(near_w)
    far_w = around(near_w, "z", 1)
    n_1, n_2, n_3 = near_x
    far_w, n_1, n_3 = lax.optimization_barrier((far_w, n_1, n_3))
    s_f0, s_f1 = around(s_p[:half], "y", 1), around(s_m[half:], "y", -1)
    far_x = along_x(far_w)
    s_f0, s_f1, n_2, *far_x = lax.optimization_barrier((s_f0, s_f1, n_2, *far_x))
    near_x = (n_1, n_2, n_3)
    o_own, o_p, o_m = (around(v, "core", 1) for v in (own, s_p, s_m))
    o_f0, o_f1 = around(s_f0, "core", 1), around(s_f1, "core", 1)
    steps, spans = [], []
    for mine, other, dy, first, tall in (
        (own, o_own, 0, 0, rows), (s_p, o_p, 3, 0, rows), (s_m, o_m, 1, 0, rows), (s_f0, o_f0, 2, 0, half), (s_f1, o_f1, 2, half, half),
    ):
        steps += [mine, other]
        spans += [(dy, 0, first, tall), (dy, 1, first, tall)]
    weight = pl.pallas_call(
        assemble_kernel,
        out_shape=jax.ShapeDtypeStruct((STEPS, Z, X, part, WIDE), gate_weight.dtype),
        in_specs=[vmem] * (Z * X),
        out_specs=vmem,
        compiler_params=pltpu.CompilerParams(vmem_limit_bytes=8 * MIB),
        name="assemble",
    )(near_w, *near_x, far_w, *far_x)
    weight = weight.reshape(deep, WIDE)

    peers = STEPS * Z * X
    rates, grad = pl.pallas_call(
        functools.partial(student_kernel, tokens_all=tokens_all, spans=spans),
        out_shape=(
            jax.ShapeDtypeStruct((rows, WIDE), jnp.float32),
            jax.ShapeDtypeStruct((peers, GROUPS * WIDE // LANES, LANES), jnp.float32),
        ),
        in_specs=[vmem] * (len(steps) + 3),
        out_specs=(vmem, vmem),
        scratch_shapes=[pltpu.VMEM((STEPS + 1, rows, WIDE), jnp.float32)],
        compiler_params=pltpu.CompilerParams(vmem_limit_bytes=12 * MIB),
        cost_estimate=pl.CostEstimate(
            flops=2 * 9 * rows * deep * WIDE, bytes_accessed=8 * MIB, transcendentals=18 * rows * WIDE
        ),
        name="student",
    )(*steps, features, weight, threshold[None])

    rates_y = [around(rates, "y", -1), around(rates, "y", 2), around(rates, "y", 1)]
    grads = lax.all_to_all(grad, ("y", "core", "z", "x"), 0, 0, tiled=True)
    pieces = [rates] + rates_y
    other = [around(v, "core", 1) for v in pieces]
    return pl.pallas_call(
        finish_kernel,
        out_shape=(
            jax.ShapeDtypeStruct((rows, width), jnp.float32),
            jax.ShapeDtypeStruct((width,), jnp.float32),
        ),
        in_specs=[vmem] * (2 * Y + 1),
        out_specs=(vmem, vmem),
        compiler_params=pltpu.CompilerParams(vmem_limit_bytes=6 * MIB),
        name="finish",
    )(*pieces, *other, grads)


def solution(mesh):
    grid = mesh.devices.reshape(Y, CORE, mesh.shape["mp"], Z, X)
    fine = Mesh(grid, ("y", "core", "mp", "z", "x"))
    tm, tok = ("y", "core"), ("z", "x")
    return jax.shard_map(
        on_device,
        mesh=fine,
        in_specs=(P(tok, None), P(tm, tok, None), P(tm + tok, "mp"), P("mp")),
        out_specs=(P(tok, "mp"), P("mp")),
        check_vma=False,
    )
```

```python
import functools
import jax
import jax.numpy as jnp
from jax import lax
from jax.experimental import pallas as pl
from jax.experimental.pallas import tpu as pltpu
from jax.sharding import Mesh, PartitionSpec as P

SHARP = 2.0
STARTS = (0, 128, 384, 640, 896, 1024, 1280, 1536)
WIDE = 256
Y, CORE, Z, X = 4, 2, 2, 4
STEPS = Y * CORE
MIB = 1024 * 1024
GROUPS = ((0, 16), (16, 32), (32, 48), (48, 64))


def around(x, axis, by):
    n = lax.axis_size(axis)
    return lax.ppermute(x, axis, [(i, (i + by) % n) for i in range(n)])


def start_of(y, core):
    w = y * CORE + core
    start = 128 * ((7 * w) // 4)
    return pl.multiple_of(start, 128)


def window_kernel(weight_ref, payload_ref):
    for w, s in enumerate(STARTS):
        payload_ref[w] = weight_ref[:, s : s + WIDE]


def assemble_kernel(*refs):
    pieces, out_ref = refs[:-1], refs[-1]
    z, x = lax.axis_index("z"), lax.axis_index("x")
    for i, piece in enumerate(pieces):
        out_ref[:, (z + i // X) % Z, (x + i % X) % X] = piece[...]


def drive_kernel(mask_hbm, features_hbm, driven_hbm, mask_ref, features_ref, driven_ref, sems):
    parts = sems.shape[0]
    tall = features_ref.shape[0] // parts
    spans = [pl.ds(i * tall, tall) for i in range(parts)]
    arriving = [
        (
            pltpu.make_async_copy(mask_hbm.at[0, at], mask_ref.at[at], sems.at[i, 0]),
            pltpu.make_async_copy(features_hbm.at[at], features_ref.at[at], sems.at[i, 1]),
        )
        for i, at in enumerate(spans)
    ]
    leaving = [pltpu.make_async_copy(driven_ref.at[at], driven_hbm.at[at], sems.at[i, 2]) for i, at in enumerate(spans)]
    for pair in arriving:
        for copy in pair:
            copy.start()
    for at, pair, out in zip(spans, arriving, leaving):
        for copy in pair:
            copy.wait()
        kept = jnp.where(mask_ref[at, :] > 0, features_ref[at, :].astype(jnp.float32), 0.0)
        driven_ref[at, :] = kept.astype(driven_ref.dtype)
        out.start()
    for out in leaving:
        out.wait()


def student_kernel(*refs, tokens_all, spans):
    count = len(spans)
    pieces, (features_ref, weight_ref, threshold_ref, rates_ref, grad_ref, current_ref) = refs[:count], refs[count:]
    rows = features_ref.shape[0]
    core, y = lax.axis_index("core"), lax.axis_index("y")
    cut = 4
    for part in (range(cut), range(cut, count)):
        last = part.stop == count
        held = [pieces[i][...] for i in part] + ([features_ref[...]] if last else [])
        total = jnp.dot(jnp.concatenate(held, axis=0), weight_ref[...], preferred_element_type=jnp.float32)
        at = 0
        for i in part:
            dy, dc, first, tall = spans[i]
            step = (y + dy) % Y * CORE + (core + dc) % CORE
            current_ref[step, first : first + tall, :] = total[at : at + tall]
            at += tall
        if last:
            current_ref[STEPS] = total[at:]
    threshold = threshold_ref[:, pl.ds(start_of(y, core), WIDE)]
    tall = GROUPS[-1][1]

    def strip(i, grad_sum):
        at = pl.ds(pl.multiple_of(i * tall, tall), tall)
        potential = jnp.zeros((tall, WIDE), jnp.float32)
        total = jnp.zeros((tall, WIDE), jnp.float32)
        for t in range(STEPS):
            rising = potential + 2.0 * current_ref[t, at, :]
            fired = jax.nn.sigmoid(SHARP * (rising - threshold))
            potential = rising - threshold * fired
            current_ref[t, at, :] = fired
            total = total + fired
        rates = threshold * total / STEPS
        rates_ref[at, :] = rates
        v = current_ref[STEPS, at, :]
        error = (rates - v * jax.nn.sigmoid(v)) / tokens_all
        share = error / STEPS
        cotangent = jnp.zeros((tall, WIDE), jnp.float32)
        for t in reversed(range(STEPS)):
            fired = current_ref[t, at, :]
            pull = share - cotangent
            dwide = pull * (SHARP * threshold) * (fired * (1.0 - fired))
            grad_sum = grad_sum + (fired * pull - dwide)
            cotangent = cotangent + dwide
        return grad_sum

    grad_sum = lax.fori_loop(0, rows // tall, strip, jnp.zeros((tall, WIDE), jnp.float32))
    for i, (first, last) in enumerate(GROUPS):
        part = jnp.sum(grad_sum[first:last], axis=0, keepdims=True)
        grad_ref[:, i * WIDE : (i + 1) * WIDE] = part


def both_kernel(mine_ref, far_ref, out_ref):
    out_ref[...] = jnp.broadcast_to((mine_ref[...] + far_ref[...])[None], out_ref.shape)


def finish_kernel(*refs):
    grads_ref, rates_ref, grad_ref = refs[-3:]
    core, y = lax.axis_index("core"), lax.axis_index("y")
    for j in range(Y):
        for k in range(CORE):
            piece = refs[Y * k + j]
            from_y, from_core = (y + j) % Y, (core + k) % CORE
            start = start_of(from_y, from_core)

            @pl.when((from_core == 0) | (from_y % 2 == 1))
            def _():
                rates_ref[:, pl.ds(start, WIDE)] = piece[...]

            @pl.when((from_core == 1) & (from_y % 2 == 0))
            def _():
                rates_ref[:, pl.ds(pl.multiple_of(start + 128, 128), WIDE - 128)] = piece[:, 128:]

    count = grads_ref.shape[0] // STEPS
    for w, s in enumerate(STARTS):
        total = jnp.sum(grads_ref[w * count : (w + 1) * count], axis=0)
        total = sum(total[:, i : i + WIDE] for i in range(0, total.shape[1], WIDE))
        skip = 128 if w % 4 == 1 else 0
        grad_ref[s + skip : s + WIDE] = total[0, skip:]


def on_device(features, spike_mask, gate_weight, threshold):
    rows, deep = features.shape
    tokens_all = rows * Z * X
    half = rows // 2
    part, width = gate_weight.shape
    vmem = pl.BlockSpec(memory_space=pltpu.VMEM)

    def along_x(held):
        return around(held, "x", -1), around(held, "x", 2), around(held, "x", 1)

    hbm = pl.BlockSpec(memory_space=pl.ANY)
    own = pl.pallas_call(
        drive_kernel,
        out_shape=jax.ShapeDtypeStruct((rows, deep), features.dtype),
        in_specs=[hbm] * 2,
        out_specs=hbm,
        scratch_shapes=[
            pltpu.VMEM((rows, deep), spike_mask.dtype),
            pltpu.VMEM((rows, deep), features.dtype),
            pltpu.VMEM((rows, deep), features.dtype),
            pltpu.SemaphoreType.DMA((4, 3)),
        ],
        compiler_params=pltpu.CompilerParams(vmem_limit_bytes=60 * MIB),
        name="drive",
    )(spike_mask, features)

    payload = pl.pallas_call(
        window_kernel,
        out_shape=jax.ShapeDtypeStruct((STEPS, part, WIDE), gate_weight.dtype),
        in_specs=[vmem],
        out_specs=vmem,
        compiler_params=pltpu.CompilerParams(vmem_limit_bytes=4 * MIB),
        name="windows",
    )(gate_weight)
    near_w = lax.all_to_all(payload, ("y", "core"), 0, 0, tiled=True)
    own, near_w = lax.optimization_barrier((own, near_w))
    s_p, s_m = around(own, "y", 1), around(own, "y", -1)
    near_x = along_x(near_w)
    far_w = around(near_w, "z", 1)
    n_1, n_2, n_3 = near_x
    far_w, n_1, n_3 = lax.optimization_barrier((far_w, n_1, n_3))
    s_f0, s_f1 = around(s_p[:half], "y", 1), around(s_m[half:], "y", -1)
    far_x = along_x(far_w)
    s_f0, s_f1, n_2, *far_x = lax.optimization_barrier((s_f0, s_f1, n_2, *far_x))
    near_x = (n_1, n_2, n_3)
    o_own, o_p, o_m = (around(v, "core", 1) for v in (own, s_p, s_m))
    o_f0, o_f1 = around(s_f0, "core", 1), around(s_f1, "core", 1)
    steps, spans = [], []
    for mine, other, dy, first, tall in (
        (own, o_own, 0, 0, rows), (s_p, o_p, 3, 0, rows), (s_m, o_m, 1, 0, rows), (s_f0, o_f0, 2, 0, half), (s_f1, o_f1, 2, half, half),
    ):
        steps += [mine, other]
        spans += [(dy, 0, first, tall), (dy, 1, first, tall)]
    weight = pl.pallas_call(
        assemble_kernel,
        out_shape=jax.ShapeDtypeStruct((STEPS, Z, X, part, WIDE), gate_weight.dtype),
        in_specs=[vmem] * (Z * X),
        out_specs=vmem,
        compiler_params=pltpu.CompilerParams(vmem_limit_bytes=8 * MIB),
        name="assemble",
    )(near_w, *near_x, far_w, *far_x)
    weight = weight.reshape(deep, WIDE)

    peers = STEPS * X
    rates, grad = pl.pallas_call(
        functools.partial(student_kernel, tokens_all=tokens_all, spans=spans),
        out_shape=(
            jax.ShapeDtypeStruct((rows, WIDE), jnp.float32),
            jax.ShapeDtypeStruct((1, len(GROUPS) * WIDE), jnp.float32),
        ),
        in_specs=[vmem] * (len(steps) + 3),
        out_specs=(vmem, vmem),
        scratch_shapes=[pltpu.VMEM((STEPS + 1, rows, WIDE), jnp.float32)],
        compiler_params=pltpu.CompilerParams(vmem_limit_bytes=12 * MIB),
        cost_estimate=pl.CostEstimate(
            flops=2 * 9 * rows * deep * WIDE, bytes_accessed=8 * MIB, transcendentals=18 * rows * WIDE
        ),
        name="student",
    )(*steps, features, weight, threshold[None])

    rates_y = [around(rates, "y", -1), around(rates, "y", 2), around(rates, "y", 1)]
    grad = pl.pallas_call(
        both_kernel,
        out_shape=jax.ShapeDtypeStruct((peers, 1, len(GROUPS) * WIDE), jnp.float32),
        in_specs=[vmem] * 2,
        out_specs=vmem,
        compiler_params=pltpu.CompilerParams(vmem_limit_bytes=4 * MIB),
        name="both",
    )(grad, around(grad, "z", 1))
    grads = lax.all_to_all(grad, ("y", "core", "x"), 0, 0, tiled=True)
    pieces = [rates] + rates_y
    other = [around(v, "core", 1) for v in pieces]
    return pl.pallas_call(
        finish_kernel,
        out_shape=(
            jax.ShapeDtypeStruct((rows, width), jnp.float32),
            jax.ShapeDtypeStruct((width,), jnp.float32),
        ),
        in_specs=[vmem] * (2 * Y + 1),
        out_specs=(vmem, vmem),
        compiler_params=pltpu.CompilerParams(vmem_limit_bytes=6 * MIB),
        name="finish",
    )(*pieces, *other, grads)


def solution(mesh):
    grid = mesh.devices.reshape(Y, CORE, mesh.shape["mp"], Z, X)
    fine = Mesh(grid, ("y", "core", "mp", "z", "x"))
    tm, tok = ("y", "core"), ("z", "x")
    return jax.shard_map(
        on_device,
        mesh=fine,
        in_specs=(P(tok, None), P(tm, tok, None), P(tm + tok, "mp"), P("mp")),
        out_specs=(P(tok, "mp"), P("mp")),
        check_vma=False,
    )
```

```python
import functools
import jax
import jax.numpy as jnp
from jax import lax
from jax.experimental import pallas as pl
from jax.experimental.pallas import tpu as pltpu
from jax.sharding import Mesh, PartitionSpec as P

SHARP = 2.0
STARTS = (0, 128, 384, 640, 896, 1024, 1280, 1536)
WIDE = 256
Y, CORE, Z, X = 4, 2, 2, 4
STEPS = Y * CORE
MIB = 1024 * 1024
GROUPS = ((0, 32), (32, 64), (64, 96), (96, 128))


def around(x, axis, by):
    n = lax.axis_size(axis)
    return lax.ppermute(x, axis, [(i, (i + by) % n) for i in range(n)])


def start_of(y, core):
    w = y * CORE + core
    start = 128 * ((7 * w) // 4)
    return pl.multiple_of(start, 128)


def window_kernel(weight_ref, payload_ref):
    for w, s in enumerate(STARTS):
        payload_ref[w] = weight_ref[:, s : s + WIDE]


def assemble_kernel(*refs):
    pieces, out_ref = refs[:-1], refs[-1]
    z, x = lax.axis_index("z"), lax.axis_index("x")
    for i, piece in enumerate(pieces):
        out_ref[:, (z + i // X) % Z, (x + i % X) % X] = piece[...]


def drive_kernel(mask_hbm, features_hbm, driven_hbm, mask_ref, features_ref, driven_ref, sems):
    parts = sems.shape[0]
    tall = features_ref.shape[0] // parts
    spans = [pl.ds(i * tall, tall) for i in range(parts)]
    arriving = [
        (
            pltpu.make_async_copy(mask_hbm.at[0, at], mask_ref.at[at], sems.at[i, 0]),
            pltpu.make_async_copy(features_hbm.at[at], features_ref.at[at], sems.at[i, 1]),
        )
        for i, at in enumerate(spans)
    ]
    leaving = [pltpu.make_async_copy(driven_ref.at[at], driven_hbm.at[at], sems.at[i, 2]) for i, at in enumerate(spans)]
    for pair in arriving:
        for copy in pair:
            copy.start()
    for at, pair, out in zip(spans, arriving, leaving):
        for copy in pair:
            copy.wait()
        kept = jnp.where(mask_ref[at, :] > 0, features_ref[at, :].astype(jnp.float32), 0.0)
        driven_ref[at, :] = kept.astype(driven_ref.dtype)
        out.start()
    for out in leaving:
        out.wait()


def student_kernel(*refs, tokens_all, spans):
    count = len(spans)
    pieces, (features_ref, weight_ref, threshold_ref, rates_ref, grad_ref, current_ref) = refs[:count], refs[count:]
    rows = features_ref.shape[0]
    core, y = lax.axis_index("core"), lax.axis_index("y")
    cut = 4
    for part in (range(cut), range(cut, count)):
        last = part.stop == count
        held = [pieces[i][...] for i in part] + ([features_ref[...]] if last else [])
        total = jnp.dot(jnp.concatenate(held, axis=0), weight_ref[...], preferred_element_type=jnp.float32)
        at = 0
        for i in part:
            dy, dc, first, tall = spans[i]
            step = (y + dy) % Y * CORE + (core + dc) % CORE
            current_ref[step, first : first + tall, :] = total[at : at + tall]
            at += tall
        if last:
            current_ref[STEPS] = total[at:]
    threshold = threshold_ref[:, pl.ds(start_of(y, core), WIDE)]
    tall = GROUPS[-1][1]

    def strip(i, grad_sum):
        at = pl.ds(pl.multiple_of(i * tall, tall), tall)
        potential = jnp.zeros((tall, WIDE), jnp.float32)
        total = jnp.zeros((tall, WIDE), jnp.float32)
        for t in range(STEPS):
            rising = potential + 2.0 * current_ref[t, at, :]
            fired = jax.nn.sigmoid(SHARP * (rising - threshold))
            potential = rising - threshold * fired
            current_ref[t, at, :] = fired
            total = total + fired
        rates = threshold * total / STEPS
        rates_ref[at, :] = rates
        v = current_ref[STEPS, at, :]
        error = (rates - v * jax.nn.sigmoid(v)) / tokens_all
        share = error / STEPS
        cotangent = jnp.zeros((tall, WIDE), jnp.float32)
        for t in reversed(range(STEPS)):
            fired = current_ref[t, at, :]
            pull = share - cotangent
            dwide = pull * (SHARP * threshold) * (fired * (1.0 - fired))
            grad_sum = grad_sum + (fired * pull - dwide)
            cotangent = cotangent + dwide
        return grad_sum

    grad_sum = lax.fori_loop(0, rows // tall, strip, jnp.zeros((tall, WIDE), jnp.float32))
    for i, (first, last) in enumerate(GROUPS):
        part = jnp.sum(grad_sum[first:last], axis=0, keepdims=True)
        grad_ref[:, i * WIDE : (i + 1) * WIDE] = part


def both_kernel(mine_ref, far_ref, out_ref):
    out_ref[...] = jnp.broadcast_to((mine_ref[...] + far_ref[...])[None], out_ref.shape)


def finish_kernel(*refs):
    grads_ref, rates_ref, grad_ref = refs[-3:]
    core, y = lax.axis_index("core"), lax.axis_index("y")
    for j in range(Y):
        for k in range(CORE):
            piece = refs[Y * k + j]
            from_y, from_core = (y + j) % Y, (core + k) % CORE
            start = start_of(from_y, from_core)

            @pl.when((from_core == 0) | (from_y % 2 == 1))
            def _():
                rates_ref[:, pl.ds(start, WIDE)] = piece[...]

            @pl.when((from_core == 1) & (from_y % 2 == 0))
            def _():
                rates_ref[:, pl.ds(pl.multiple_of(start + 128, 128), WIDE - 128)] = piece[:, 128:]

    count = grads_ref.shape[0] // STEPS
    for w, s in enumerate(STARTS):
        total = jnp.sum(grads_ref[w * count : (w + 1) * count], axis=0)
        total = sum(total[:, i : i + WIDE] for i in range(0, total.shape[1], WIDE))
        skip = 128 if w % 4 == 1 else 0
        grad_ref[s + skip : s + WIDE] = total[0, skip:]


def on_device(features, spike_mask, gate_weight, threshold):
    rows, deep = features.shape
    tokens_all = rows * Z * X
    half = rows // 2
    part, width = gate_weight.shape
    vmem = pl.BlockSpec(memory_space=pltpu.VMEM)

    def along_x(held):
        return around(held, "x", -1), around(held, "x", 2), around(held, "x", 1)

    hbm = pl.BlockSpec(memory_space=pl.ANY)
    own = pl.pallas_call(
        drive_kernel,
        out_shape=jax.ShapeDtypeStruct((rows, deep), features.dtype),
        in_specs=[hbm] * 2,
        out_specs=hbm,
        scratch_shapes=[
            pltpu.VMEM((rows, deep), spike_mask.dtype),
            pltpu.VMEM((rows, deep), features.dtype),
            pltpu.VMEM((rows, deep), features.dtype),
            pltpu.SemaphoreType.DMA((4, 3)),
        ],
        compiler_params=pltpu.CompilerParams(vmem_limit_bytes=60 * MIB),
        name="drive",
    )(spike_mask, features)

    payload = pl.pallas_call(
        window_kernel,
        out_shape=jax.ShapeDtypeStruct((STEPS, part, WIDE), gate_weight.dtype),
        in_specs=[vmem],
        out_specs=vmem,
        compiler_params=pltpu.CompilerParams(vmem_limit_bytes=4 * MIB),
        name="windows",
    )(gate_weight)
    near_w = lax.all_to_all(payload, ("y", "core"), 0, 0, tiled=True)
    own, near_w = lax.optimization_barrier((own, near_w))
    s_p, s_m = around(own, "y", 1), around(own, "y", -1)
    near_x = along_x(near_w)
    far_w = around(near_w, "z", 1)
    n_1, n_2, n_3 = near_x
    far_w, n_1, n_3 = lax.optimization_barrier((far_w, n_1, n_3))
    s_f0, s_f1 = around(s_p[:half], "y", 1), around(s_m[half:], "y", -1)
    far_x = along_x(far_w)
    s_f0, s_f1, n_2, *far_x = lax.optimization_barrier((s_f0, s_f1, n_2, *far_x))
    near_x = (n_1, n_2, n_3)
    o_own, o_p, o_m = (around(v, "core", 1) for v in (own, s_p, s_m))
    o_f0, o_f1 = around(s_f0, "core", 1), around(s_f1, "core", 1)
    steps, spans = [], []
    for mine, other, dy, first, tall in (
        (own, o_own, 0, 0, rows), (s_p, o_p, 3, 0, rows), (s_m, o_m, 1, 0, rows), (s_f0, o_f0, 2, 0, half), (s_f1, o_f1, 2, half, half),
    ):
        steps += [mine, other]
        spans += [(dy, 0, first, tall), (dy, 1, first, tall)]
    weight = pl.pallas_call(
        assemble_kernel,
        out_shape=jax.ShapeDtypeStruct((STEPS, Z, X, part, WIDE), gate_weight.dtype),
        in_specs=[vmem] * (Z * X),
        out_specs=vmem,
        compiler_params=pltpu.CompilerParams(vmem_limit_bytes=8 * MIB),
        name="assemble",
    )(near_w, *near_x, far_w, *far_x)
    weight = weight.reshape(deep, WIDE)

    peers = STEPS * X
    rates, grad = pl.pallas_call(
        functools.partial(student_kernel, tokens_all=tokens_all, spans=spans),
        out_shape=(
            jax.ShapeDtypeStruct((rows, WIDE), jnp.float32),
            jax.ShapeDtypeStruct((1, len(GROUPS) * WIDE), jnp.float32),
        ),
        in_specs=[vmem] * (len(steps) + 3),
        out_specs=(vmem, vmem),
        scratch_shapes=[pltpu.VMEM((STEPS + 1, rows, WIDE), jnp.float32)],
        compiler_params=pltpu.CompilerParams(vmem_limit_bytes=12 * MIB),
        cost_estimate=pl.CostEstimate(
            flops=2 * 9 * rows * deep * WIDE, bytes_accessed=8 * MIB, transcendentals=18 * rows * WIDE
        ),
        name="student",
    )(*steps, features, weight, threshold[None])

    rates_y = [around(rates, "y", -1), around(rates, "y", 2), around(rates, "y", 1)]
    grad = pl.pallas_call(
        both_kernel,
        out_shape=jax.ShapeDtypeStruct((peers, 1, len(GROUPS) * WIDE), jnp.float32),
        in_specs=[vmem] * 2,
        out_specs=vmem,
        compiler_params=pltpu.CompilerParams(vmem_limit_bytes=4 * MIB),
        name="both",
    )(grad, around(grad, "z", 1))
    grads = lax.all_to_all(grad, ("y", "core", "x"), 0, 0, tiled=True)
    pieces = [rates] + rates_y
    other = [around(v, "core", 1) for v in pieces]
    return pl.pallas_call(
        finish_kernel,
        out_shape=(
            jax.ShapeDtypeStruct((rows, width), jnp.float32),
            jax.ShapeDtypeStruct((width,), jnp.float32),
        ),
        in_specs=[vmem] * (2 * Y + 1),
        out_specs=(vmem, vmem),
        compiler_params=pltpu.CompilerParams(vmem_limit_bytes=6 * MIB),
        name="finish",
    )(*pieces, *other, grads)


def solution(mesh):
    grid = mesh.devices.reshape(Y, CORE, mesh.shape["mp"], Z, X)
    fine = Mesh(grid, ("y", "core", "mp", "z", "x"))
    tm, tok = ("y", "core"), ("z", "x")
    return jax.shard_map(
        on_device,
        mesh=fine,
        in_specs=(P(tok, None), P(tm, tok, None), P(tm + tok, "mp"), P("mp")),
        out_specs=(P(tok, "mp"), P("mp")),
        check_vma=False,
    )
```
